128 devices in a mesh: grp: 4 (over x), bulk: 32 (over y, z, core).
Axes of the slice: x: 4, y: 4, z: 4, core: 2. Of those that a mesh axis runs over, the one named last changes fastest.
Arguments:
- embeddings: bfloat16 [49152, 768], P(('grp', 'bulk')), may hold values from -100 to 100
- cluster_ids: int32 [49152], P(('grp', 'bulk')), may hold values from 0 to 255, as said below
Outputs:
- redundancy: float32 [49152], P(('grp', 'bulk'))
The draws below stay inside these ranges and needn't reach their ends.
Inputs may be any that keep to these rules, and one draw needn't show every extreme that they name: `cluster_ids`: the cluster group of a row is its id // 64; every aligned block of 384 rows holds exactly 96 rows of each cluster group.
All inputs are finite; a program needn't handle non-finite values.
Results may differ from the reference program's by a relative error of at most 0.0015.
Values may be sent and summed in bfloat16 or wider, within the bound.
No kernel may reach another device: no remote copies, remote signals or barrier semaphores. Data moves between devices by JAX's collectives and lax.ppermute only.
A program may use at most 64 MiB of HBM per device.

```python
import math
import jax
import jax.numpy as jnp
from jax import lax

D = 768
ROW_DEV = 384
CL_GRP = 64
CLUSTERS = 256
ROWS = 49152
N_GRP = 4
DEVICES = 128


def cluster_table(key):
    key = jax.random.fold_in(key, 11)
    k_grp, k_upper, k_pick, k_perm = jax.random.split(key, 4)
    share = ROW_DEV // N_GRP
    base = jnp.repeat(jnp.arange(N_GRP, dtype=jnp.int32), share)
    groups = jax.vmap(lambda k: jax.random.permutation(k, base))(jax.random.split(k_grp, DEVICES)).reshape(ROWS)
    upper = jax.random.randint(k_upper, (ROWS,), 1, CL_GRP + 1)
    picked = jax.random.randint(k_pick, (ROWS,), 0, 1 << 20) % upper
    labels = jax.random.permutation(k_perm, CL_GRP).astype(jnp.int32)[picked]
    first_low = jnp.argmax(groups == 0)
    first_high = jnp.argmax(groups == N_GRP - 1)
    labels = labels.at[first_low].set(0).at[first_high].set(CL_GRP - 1)
    return (groups * CL_GRP + labels).astype(jnp.int32)


def draw_cluster_ids(key, part):
    return cluster_table(key)


def draw_embeddings(key, part):
    labels = cluster_table(key)
    key = jax.random.fold_in(key, 23)
    k_center, k_offset, k_mix, k_noise, k_spread, k_magnitude = jax.random.split(key, 6)
    group_mean = jax.random.normal(k_center, (N_GRP, D), jnp.float32)
    offsets = jax.random.normal(k_offset, (CLUSTERS, D), jnp.float32)
    mixing = jax.random.uniform(k_mix, (CLUSTERS, 1), jnp.float32, 0.7, 0.9)
    group_of = jnp.arange(CLUSTERS, dtype=jnp.int32) // CL_GRP
    centers = jnp.sqrt(mixing) * group_mean[group_of] + jnp.sqrt(1.0 - mixing) * offsets
    noise = jax.random.normal(k_noise, (ROWS, D), jnp.float32)
    spread = jnp.exp(jax.random.uniform(k_spread, (ROWS, 1), jnp.float32, math.log(0.05), math.log(1.5)))
    magnitude = jnp.exp(jax.random.uniform(k_magnitude, (ROWS, 1), jnp.float32, math.log(0.5), math.log(4.0)))
    return (magnitude * (centers[labels] + spread * noise)).astype(jnp.bfloat16)


def setup_inputs(seed: int = 0) -> dict:
    streams_of = jax.random.split(jax.random.key(seed), 3)
    embeddings = draw_embeddings(jax.random.fold_in(streams_of[2], 71), 0)
    cluster_ids = draw_cluster_ids(jax.random.fold_in(streams_of[2], 71), 0)
    return dict(embeddings=embeddings, cluster_ids=cluster_ids)


TEMP = 0.05

def unit_rows(embeddings):
    values = embeddings.astype(jnp.float32)
    scale = lax.rsqrt(lax.optimization_barrier(jnp.sum(values * values, axis=1, keepdims=True)) + 1e-06)
    return (values * scale).astype(jnp.bfloat16)

def reference(embeddings, cluster_ids):
    units = unit_rows(embeddings)
    groups = cluster_ids // CL_GRP
    order = jnp.argsort(groups, stable=True).astype(jnp.int32)
    group_rows = ROWS // N_GRP
    sorted_units = units[order].reshape(N_GRP, group_rows, D)
    sorted_ids = cluster_ids[order].reshape(N_GRP, group_rows)
    places = jnp.arange(group_rows, dtype=jnp.int32)

    def per_group(pair):
        keys = pair[0].astype(jnp.float32)
        key_ids = pair[1]

        def per_block(index):
            start = (index * ROW_DEV).astype(jnp.int32)
            queries = lax.dynamic_slice_in_dim(keys, start, ROW_DEV, 0)
            query_ids = lax.dynamic_slice_in_dim(key_ids, start, ROW_DEV, 0)
            similarity = jnp.dot(queries, keys.T, precision=lax.Precision.HIGHEST)
            rows_here = start + jnp.arange(ROW_DEV, dtype=jnp.int32)
            keep = (query_ids[:, None] == key_ids[None, :]) & (rows_here[:, None] != places[None, :])
            terms = jnp.where(keep, jnp.exp((similarity - 1.0) / TEMP), jnp.float32(0.0))
            return jnp.log1p(lax.optimization_barrier(jnp.sum(terms, axis=1)))
        return lax.map(per_block, jnp.arange(group_rows // ROW_DEV, dtype=jnp.int32)).reshape(group_rows)
    scores = lax.map(per_group, (sorted_units, sorted_ids)).reshape(ROWS)
    return jnp.zeros((ROWS,), jnp.float32).at[order].set(scores)
```

```python
import functools

import jax
import jax.numpy as jnp
import numpy as np
from jax import lax
from jax.experimental import pallas as pl
from jax.experimental.pallas import tpu as pltpu
from jax.sharding import Mesh
from jax.sharding import PartitionSpec as P

CL_GRP = 64
GROUPS = 4
TEMP = 0.05
RATE = 1.4426950408889634 / TEMP
AXES = ("x", "y", "z", "c")
SIZES = (4, 4, 4, 2)
TAIL = 16
VMEM_LIMIT = 48 * 1024 * 1024


def iotas(rows, cols):
    return (
        lax.broadcasted_iota(jnp.int32, (rows, cols), 0),
        lax.broadcasted_iota(jnp.int32, (rows, cols), 1),
    )


def as_column(row):
    n = row.shape[1]
    down, across = iotas(n, n)
    return jnp.sum(jnp.where(down == across, row, 0.0), axis=1, keepdims=True)


def prepare_kernel(x_ref, emb_ref, ids_ref, c0_ref, c1_ref, c2_ref, c3_ref, pos_ref):
    rows = emb_ref.shape[0]
    share = rows // GROUPS
    values = emb_ref[...].astype(jnp.float32)
    scale = lax.rsqrt(jnp.sum(values * values, axis=1, keepdims=True) + 1e-06)
    units = (values * scale).astype(jnp.bfloat16)
    ids = ids_ref[...]
    down, across = iotas(rows, rows)
    steps = (lax.shift_right_logical(ids, 6) - x_ref[0]) & (GROUPS - 1)
    key = (steps * rows + across[:1]).astype(jnp.float32)
    pos = jnp.sum(jnp.where(as_column(key) < key, 1.0, 0.0), axis=0, keepdims=True)
    pos_ref[...] = pos
    place = jnp.where(down.astype(jnp.float32) == pos, 1.0, 0.0).astype(jnp.bfloat16)
    placed = jnp.dot(place, units, preferred_element_type=jnp.float32).astype(jnp.bfloat16)
    wide = jnp.broadcast_to(ids.astype(jnp.float32), (TAIL, rows)).astype(jnp.bfloat16)
    placed_ids = lax.dot_general(
        wide, place, (((1,), (1,)), ((), ())), preferred_element_type=jnp.float32
    )
    chunk_of = lax.broadcasted_iota(jnp.int32, (TAIL, rows), 1)
    for k, out in enumerate((c0_ref, c1_ref, c2_ref, c3_ref)):
        out[:share, :] = placed[k * share : (k + 1) * share]
        here = (chunk_of >= k * share) & (chunk_of < (k + 1) * share)
        out[share:, :rows] = jnp.where(here, placed_ids, 0.0).astype(jnp.bfloat16)
        out[share:, rows:] = jnp.zeros((TAIL, out.shape[1] - rows), jnp.bfloat16)


def prepare(x_index, embeddings, ids):
    rows, width = embeddings.shape
    share = rows // GROUPS
    chunk = jax.ShapeDtypeStruct((share + TAIL, width), jnp.bfloat16)
    return pl.pallas_call(
        prepare_kernel,
        out_shape=[chunk] * GROUPS + [jax.ShapeDtypeStruct((1, rows), jnp.float32)],
        in_specs=[
            pl.BlockSpec(memory_space=pltpu.SMEM),
            pl.BlockSpec(memory_space=pltpu.VMEM),
            pl.BlockSpec(memory_space=pltpu.VMEM),
        ],
        compiler_params=pltpu.CompilerParams(vmem_limit_bytes=VMEM_LIMIT),
        name="prepare",
    )(x_index, embeddings, ids)


def join_kernel(c0_ref, c1_ref, c2_ref, c3_ref, out_ref):
    chunks = (c0_ref, c1_ref, c2_ref, c3_ref)
    share = c0_ref.shape[0] - TAIL
    tail = 0.0
    for k, chunk in enumerate(chunks):
        out_ref[k * share : (k + 1) * share, :] = chunk[:share, :]
        tail += chunk[share:, :].astype(jnp.float32)
    out_ref[GROUPS * share :, :] = tail.astype(jnp.bfloat16)


def join(chunks):
    share = chunks[0].shape[0] - TAIL
    return pl.pallas_call(
        join_kernel,
        out_shape=jax.ShapeDtypeStruct((GROUPS * share + TAIL, chunks[0].shape[1]), jnp.bfloat16),
        compiler_params=pltpu.CompilerParams(vmem_limit_bytes=VMEM_LIMIT),
        name="join",
    )(*chunks)


def pairs_kernel(nq, nk, plan, same, *refs):
    queries, keys = refs[:nq], refs[nq : nq + nk]
    out_ref, q_buf, k_buf, q_ids, k_ids, acc, sems = refs[nq + nk :]
    rows = q_ids.shape[2]
    copies = {}

    def fetch(kind, index):
        if (kind, index) in copies:
            return
        source, rows_buf, ids_buf = (
            (queries[index], q_buf, q_ids) if kind == "q" else (keys[index], k_buf, k_ids)
        )
        slot = 2 * (index if kind == "q" else nq + index)
        pair = [
            pltpu.make_async_copy(
                source.at[pl.ds(0, rows), :], rows_buf.at[pl.ds(index * rows, rows), :], sems.at[slot]
            ),
            pltpu.make_async_copy(
                source.at[pl.ds(rows, TAIL), pl.ds(0, rows)], ids_buf.at[index], sems.at[slot + 1]
            ),
        ]
        for copy in pair:
            copy.start()
        copies[kind, index] = pair

    for k, first, count in plan:
        for q in range(first, first + count):
            fetch("q", q)
        fetch("k", k)
    acc[...] = jnp.zeros_like(acc)
    done = set()

    def arrived(kind, index):
        if (kind, index) not in done:
            done.add((kind, index))
            for copy in copies[kind, index]:
                copy.wait()

    for step, (k, first, count) in enumerate(plan):
        for q in range(first, first + count):
            arrived("q", q)
        arrived("k", k)
        id_row = k_ids[k][:1].astype(jnp.float32)
        key_ids = jnp.transpose(jnp.broadcast_to(id_row, (128, rows)))
        key_rows = k_buf[k * rows : (k + 1) * rows, :]
        at = first
        while at < first + count:
            n = min(2, first + count - at)
            similarity = lax.dot_general(
                key_rows,
                q_buf[at * rows : (at + n) * rows, :],
                (((1,), (1,)), ((), ())),
                preferred_element_type=jnp.float32,
            )
            for q in range(at, at + n):
                query_ids = q_ids[q][:1].astype(jnp.float32)
                for lane in range(0, rows, 128):
                    col = (q - at) * rows + lane
                    tile = similarity[:, col : col + 128]
                    keep = key_ids == query_ids[:, lane : lane + 128]
                    if step == same:
                        down, across = iotas(rows, 128)
                        keep = keep & (down != across + lane)
                    terms = jnp.where(keep, jnp.exp2((tile - 1.0) * RATE), 0.0)
                    acc[:, q * rows + lane : q * rows + lane + 128] += jnp.sum(
                        terms.reshape(rows // 8, 8, 128), axis=0
                    )
            at += n
    for q in range(nq):
        out_ref[q] = jnp.sum(acc[:, q * rows : (q + 1) * rows], axis=0, keepdims=True)


def pair_sums(queries, keys, plan, same=None, name="pairs"):
    rows, width = queries[0].shape[0] - TAIL, queries[0].shape[1]
    nq, nk = len(queries), len(keys)
    products = sum(count for _, _, count in plan) * rows * rows
    return pl.pallas_call(
        functools.partial(pairs_kernel, nq, nk, plan, same),
        out_shape=jax.ShapeDtypeStruct((nq, 1, rows), jnp.float32),
        in_specs=[pl.BlockSpec(memory_space=pl.ANY)] * (nq + nk),
        out_specs=pl.BlockSpec(memory_space=pltpu.VMEM),
        scratch_shapes=[
            pltpu.VMEM((nq * rows, width), jnp.bfloat16),
            pltpu.VMEM((nk * rows, width), jnp.bfloat16),
            pltpu.VMEM((nq, TAIL, rows), jnp.bfloat16),
            pltpu.VMEM((nk, TAIL, rows), jnp.bfloat16),
            pltpu.VMEM((8, nq * rows), jnp.float32),
            pltpu.SemaphoreType.DMA((2 * (nq + nk),)),
        ],
        compiler_params=pltpu.CompilerParams(vmem_limit_bytes=VMEM_LIMIT),
        cost_estimate=pl.CostEstimate(
            flops=2 * products * width,
            bytes_accessed=(nq + nk) * rows * width * 2,
            transcendentals=products,
        ),
        name=name,
    )(*queries, *keys)


def finish_kernel(pos_ref, m0_ref, m1_ref, m2_ref, m3_ref, out_ref):
    rows = pos_ref.shape[1]
    share = rows // GROUPS
    lane = lax.broadcasted_iota(jnp.int32, (1, rows), 1)
    masses = m0_ref[...]
    for k, ref in enumerate((m1_ref, m2_ref, m3_ref), 1):
        masses = jnp.where(lane >= k * share, ref[...], masses)
    down, _ = iotas(rows, rows)
    picked = jnp.where(down.astype(jnp.float32) == pos_ref[...], as_column(masses), 0.0)
    out_ref[...] = jnp.log1p(jnp.sum(picked, axis=0, keepdims=True))


def finish(pos, masses):
    return pl.pallas_call(
        finish_kernel,
        out_shape=jax.ShapeDtypeStruct(pos.shape, jnp.float32),
        compiler_params=pltpu.CompilerParams(vmem_limit_bytes=VMEM_LIMIT),
        name="finish",
    )(pos, *masses)


def pairs_of(source_of):
    moves = []
    for here in np.ndindex(*SIZES):
        there = tuple(int(v) % n for v, n in zip(source_of(*here), SIZES))
        moves.append((int(np.ravel_multi_index(there, SIZES)), int(np.ravel_multi_index(here, SIZES))))
    return moves


def receive(array, source_of):
    return lax.ppermute(array, AXES, pairs_of(source_of))


def side(c):
    return -1 if c == 0 else 1


def swap(a):
    return receive(a, lambda x, y, z, c: (x, y, z, 1 - c))


def near_y(a):
    return receive(a, lambda x, y, z, c: (x, y + side(c), z, c))


def near_z(a):
    return receive(a, lambda x, y, z, c: (x, y, z + side(c), c))


def shards(embeddings, cluster_ids):
    rows = embeddings.shape[0]
    x_index = lax.axis_index("x").astype(jnp.int32).reshape(1)
    *chunks, pos = prepare(x_index, embeddings, cluster_ids.reshape(1, rows))
    for k in range(1, GROUPS):
        chunks[k] = receive(chunks[k], lambda x, y, z, c, k=k: (x - k, y, z, c))
    own = join(chunks)

    az, ay = near_z(own), near_y(own)
    other = swap(own)
    bz, by = near_z(other), near_y(other)
    fz, fy = near_z(az), near_y(ay)
    ay2, by2, fy2 = swap(ay), swap(by), swap(fy)

    s0 = pair_sums([own], [own, other], ((0, 0, 1), (1, 0, 1)), same=0, name="pairs_own")
    s1 = pair_sums(
        [own, az], [ay, ay2, own, other], ((0, 0, 2), (1, 0, 2), (2, 1, 1), (3, 1, 1)), name="pairs_a"
    )
    s2 = pair_sums(
        [own, az, bz],
        [by, by2, own, other, ay, ay2],
        ((0, 0, 3), (1, 0, 3), (2, 2, 1), (3, 2, 1), (4, 2, 1), (5, 2, 1)),
        name="pairs_b",
    )
    s3 = pair_sums(
        [own, az, bz, fz],
        [fy, fy2, own, other, ay, ay2, by, by2],
        ((2, 3, 1), (3, 3, 1), (4, 3, 1), (5, 3, 1), (6, 3, 1), (7, 3, 1), (0, 0, 4), (1, 0, 4)),
        name="pairs_f",
    )
    mass = s0[0] + s1[0] + s2[0] + s3[0]
    mass_a = s1[1] + s2[1] + s3[1]
    mass_b = s2[2] + s3[2]
    mass_f = s3[3]
    mass = (
        mass
        + receive(mass_a, lambda x, y, z, c: (x, y, z - side(c), c))
        + receive(mass_b, lambda x, y, z, c: (x, y, z + side(c), 1 - c))
        + receive(mass_f, lambda x, y, z, c: (x, y, z + 2, c))
    )
    masses = [mass] + [
        receive(mass, lambda x, y, z, c, k=k: (x + k, y, z, c)) for k in range(1, GROUPS)
    ]
    return finish(pos, masses).reshape(rows)


def solution(mesh):
    devices = Mesh(np.asarray(mesh.devices).reshape(SIZES), AXES)
    return jax.shard_map(
        shards, mesh=devices, in_specs=(P(AXES, None), P(AXES)), out_specs=P(AXES), check_vma=False
    )
```

```python
import functools

import jax
import jax.numpy as jnp
import numpy as np
from jax import lax
from jax.experimental import pallas as pl
from jax.experimental.pallas import tpu as pltpu
from jax.sharding import Mesh
from jax.sharding import PartitionSpec as P

CL_GRP = 64
GROUPS = 4
TEMP = 0.05
RATE = 1.4426950408889634 / TEMP
STEPS = (0, 1, 3, 2)
AXES = ("x", "y", "z", "c")
SIZES = (4, 4, 4, 2)
TAIL = 16
VMEM_LIMIT = 32 * 1024 * 1024


def iotas(rows, cols):
    return (
        lax.broadcasted_iota(jnp.int32, (rows, cols), 0),
        lax.broadcasted_iota(jnp.int32, (rows, cols), 1),
    )


def as_column(row):
    n = row.shape[1]
    down, across = iotas(n, n)
    return jnp.sum(jnp.where(down == across, row, 0.0), axis=1, keepdims=True)


def prepare_kernel(x_ref, emb_ref, ids_ref, c0_ref, c1_ref, c3_ref, c2_ref, pos_ref):
    rows = emb_ref.shape[0]
    share = rows // GROUPS
    values = emb_ref[...].astype(jnp.float32)
    scale = lax.rsqrt(jnp.sum(values * values, axis=1, keepdims=True) + 1e-06)
    units = (values * scale).astype(jnp.bfloat16)
    ids = ids_ref[...]
    down, across = iotas(rows, rows)
    steps = (lax.shift_right_logical(ids, 6) - x_ref[0]) & (GROUPS - 1)
    slot = steps ^ lax.shift_right_logical(steps, 1)
    key = (slot * rows + across[:1]).astype(jnp.float32)
    pos = jnp.sum(jnp.where(as_column(key) < key, 1.0, 0.0), axis=0, keepdims=True)
    pos_ref[...] = pos
    place = jnp.where(down.astype(jnp.float32) == pos, 1.0, 0.0).astype(jnp.bfloat16)
    placed = jnp.dot(place, units, preferred_element_type=jnp.float32).astype(jnp.bfloat16)
    wide = jnp.broadcast_to(ids.astype(jnp.float32), (TAIL, rows)).astype(jnp.bfloat16)
    placed_ids = lax.dot_general(
        wide, place, (((1,), (1,)), ((), ())), preferred_element_type=jnp.float32
    )
    chunk_of = lax.broadcasted_iota(jnp.int32, (TAIL, rows), 1)
    for k, out in enumerate((c0_ref, c1_ref, c3_ref, c2_ref)):
        out[:share, :] = placed[k * share : (k + 1) * share]
        here = (chunk_of >= k * share) & (chunk_of < (k + 1) * share)
        out[share:, :rows] = jnp.where(here, placed_ids, 0.0).astype(jnp.bfloat16)
        out[share:, rows:] = jnp.zeros((TAIL, out.shape[1] - rows), jnp.bfloat16)


def prepare(x_index, embeddings, ids):
    rows, width = embeddings.shape
    share = rows // GROUPS
    chunk = jax.ShapeDtypeStruct((share + TAIL, width), jnp.bfloat16)
    return pl.pallas_call(
        prepare_kernel,
        out_shape=[chunk] * GROUPS + [jax.ShapeDtypeStruct((1, rows), jnp.float32)],
        in_specs=[
            pl.BlockSpec(memory_space=pltpu.SMEM),
            pl.BlockSpec(memory_space=pltpu.VMEM),
            pl.BlockSpec(memory_space=pltpu.VMEM),
        ],
        compiler_params=pltpu.CompilerParams(vmem_limit_bytes=VMEM_LIMIT),
        name="prepare",
    )(x_index, embeddings, ids)


def join_kernel(c0_ref, c1_ref, c2_ref, c3_ref, out_ref):
    chunks = (c0_ref, c1_ref, c2_ref, c3_ref)
    share = c0_ref.shape[0] - TAIL
    tail = 0.0
    for k, chunk in enumerate(chunks):
        out_ref[k * share : (k + 1) * share, :] = chunk[:share, :]
        tail += chunk[share:, :].astype(jnp.float32)
    out_ref[GROUPS * share :, :] = tail.astype(jnp.bfloat16)


def join(chunks):
    share = chunks[0].shape[0] - TAIL
    return pl.pallas_call(
        join_kernel,
        out_shape=jax.ShapeDtypeStruct((GROUPS * share + TAIL, chunks[0].shape[1]), jnp.bfloat16),
        compiler_params=pltpu.CompilerParams(vmem_limit_bytes=VMEM_LIMIT),
        name="join",
    )(*chunks)


def pairs_kernel(nq, nk, plan, *refs):
    queries, keys = refs[:nq], refs[nq : nq + nk]
    out_ref, down_acc, across_acc = refs[nq + nk :]
    rows = out_ref.shape[2]
    down_acc[...] = jnp.zeros_like(down_acc)
    across_acc[...] = jnp.zeros_like(across_acc)

    def id_rows(blocks):
        return [block[rows:, :rows][:1].astype(jnp.float32) for block in blocks]

    def id_column(block):
        return jnp.transpose(jnp.broadcast_to(id_rows([block])[0], (128, rows)))

    def similar(tall, wide):
        parts = [block[:rows, :] for block in wide]
        return lax.dot_general(
            tall[:rows, :],
            jnp.concatenate(parts, axis=0) if len(parts) > 1 else parts[0],
            (((1,), (1,)), ((), ())),
            preferred_element_type=jnp.float32,
        )

    def term(similarity, keep):
        return jnp.where(keep, jnp.exp2((similarity - 1.0) * RATE), 0.0)

    for qs, ks, *same in plan:
        if len(ks) == 1:
            similarity = similar(keys[ks[0]], [queries[q] for q in qs])
            key_ids = id_column(keys[ks[0]])
            for i, (q, query_ids) in enumerate(zip(qs, id_rows([queries[q] for q in qs]))):
                for lane in range(0, rows, 128):
                    tile = similarity[:, i * rows + lane : i * rows + lane + 128]
                    terms = term(tile, key_ids == query_ids[:, lane : lane + 128])
                    down_acc[:, q * rows + lane : q * rows + lane + 128] += jnp.sum(
                        terms.reshape(rows // 8, 8, 128), axis=0
                    )
        else:
            (q,) = qs
            similarity = similar(queries[q], [keys[k] for k in ks])
            query_ids = id_column(queries[q])
            total = across_acc[q]
            for i, key_ids in enumerate(id_rows([keys[k] for k in ks])):
                for lane in range(0, rows, 128):
                    tile = similarity[:, i * rows + lane : i * rows + lane + 128]
                    keep = query_ids == key_ids[:, lane : lane + 128]
                    if same and i == 0:
                        down, across = iotas(rows, 128)
                        keep = keep & (down != across + lane)
                    total += term(tile, keep)
            across_acc[q] = total
    across_used = {qs[0] for qs, ks, *_ in plan if len(ks) > 1}
    for q in range(nq):
        total = jnp.sum(down_acc[:, q * rows : (q + 1) * rows], axis=0, keepdims=True)
        if q in across_used:
            total += jnp.sum(jnp.transpose(across_acc[q]), axis=0, keepdims=True)
        out_ref[q] = total


def pair_sums(queries, keys, plan, name):
    rows, width = queries[0].shape[0] - TAIL, queries[0].shape[1]
    nq, nk = len(queries), len(keys)
    products = sum(len(qs) * len(ks) for qs, ks, *_ in plan) * rows * rows
    return pl.pallas_call(
        functools.partial(pairs_kernel, nq, nk, plan),
        out_shape=jax.ShapeDtypeStruct((nq, 1, rows), jnp.float32),
        in_specs=[pl.BlockSpec(memory_space=pltpu.VMEM)] * (nq + nk),
        out_specs=pl.BlockSpec(memory_space=pltpu.VMEM),
        scratch_shapes=[
            pltpu.VMEM((8, nq * rows), jnp.float32),
            pltpu.VMEM((nq, rows, 128), jnp.float32),
        ],
        compiler_params=pltpu.CompilerParams(vmem_limit_bytes=VMEM_LIMIT),
        cost_estimate=pl.CostEstimate(
            flops=2 * products * width,
            bytes_accessed=(nq + nk) * rows * width * 2,
            transcendentals=products,
        ),
        name=name,
    )(*queries, *keys)


def finish_kernel(pos_ref, m0_ref, m1_ref, m2_ref, m3_ref, out_ref):
    rows = pos_ref.shape[1]
    share = rows // GROUPS
    lane = lax.broadcasted_iota(jnp.int32, (1, rows), 1)
    masses = m0_ref[...]
    for k, ref in enumerate((m1_ref, m2_ref, m3_ref), 1):
        masses = jnp.where(lane >= k * share, ref[...], masses)
    down, _ = iotas(rows, rows)
    picked = jnp.where(down.astype(jnp.float32) == pos_ref[...], as_column(masses), 0.0)
    out_ref[...] = jnp.log1p(jnp.sum(picked, axis=0))


def finish(pos, masses):
    return pl.pallas_call(
        finish_kernel,
        out_shape=jax.ShapeDtypeStruct((pos.shape[1],), jnp.float32),
        compiler_params=pltpu.CompilerParams(vmem_limit_bytes=VMEM_LIMIT),
        name="finish",
    )(pos, *masses)


def pairs_of(source_of):
    moves = []
    for here in np.ndindex(*SIZES):
        there = tuple(int(v) % n for v, n in zip(source_of(*here), SIZES))
        moves.append((int(np.ravel_multi_index(there, SIZES)), int(np.ravel_multi_index(here, SIZES))))
    return moves


def receive(array, source_of):
    return lax.ppermute(array, AXES, pairs_of(source_of))


def side(c):
    return -1 if c == 0 else 1


def swap(a):
    return receive(a, lambda x, y, z, c: (x, y, z, 1 - c))


def near_y(a):
    return receive(a, lambda x, y, z, c: (x, y + side(c), z, c))


def near_z(a):
    return receive(a, lambda x, y, z, c: (x, y, z + side(c), c))


def shards(embeddings, cluster_ids):
    rows = embeddings.shape[0]
    x_index = lax.axis_index("x").astype(jnp.int32).reshape(1)
    *chunks, pos = prepare(x_index, embeddings, cluster_ids.reshape(1, rows))
    for k, step in enumerate(STEPS):
        if step:
            chunks[k] = receive(chunks[k], lambda x, y, z, c, step=step: (x - step, y, z, c))
    own = join(chunks)

    ay, az = lax.optimization_barrier((near_y(own), near_z(own)))
    other = swap(own)
    fz, fy = near_z(az), near_y(ay)
    bz, by = near_z(other), near_y(other)
    by, bz = lax.optimization_barrier((by, bz))
    ay2, by2 = swap(ay), swap(by)
    s1 = pair_sums(
        [az, bz, own],
        [own, other, ay, ay2, by],
        (
            ((0, 1), (0,)),
            ((0, 1), (1,)),
            ((0, 1), (2,)),
            ((0, 1), (3,)),
            ((0, 1), (4,)),
            ((2,), (0, 1), True),
            ((2,), (2, 3)),
        ),
        name="pairs_a",
    )
    fy, fz, s1 = lax.optimization_barrier((fy, fz, s1))
    fy2 = swap(fy)
    s2 = pair_sums(
        [az, bz, fz],
        [by2, own, other, ay, ay2, by],
        (((0, 1), (0,)), ((2,), (1, 2)), ((2,), (3, 4)), ((2,), (5, 0))),
        name="pairs_b",
    )
    s3 = pair_sums(
        [az, bz, fz], [fy, fy2], (((0, 1), (0,)), ((0, 1), (1,)), ((2,), (0, 1))), name="pairs_f"
    )
    s0 = pair_sums([own], [by, by2, fy, fy2], (((0,), (0, 1)), ((0,), (2, 3))), name="pairs_own")
    mass_a = s1[0] + s2[0] + s3[0]
    mass_b = s1[1] + s2[1] + s3[1]
    mass_f = s2[2] + s3[2]
    mass = (
        s0[0]
        + s1[2]
        + receive(mass_f, lambda x, y, z, c: (x, y, z + 2, c))
        + receive(mass_a, lambda x, y, z, c: (x, y, z - side(c), c))
        + receive(mass_b, lambda x, y, z, c: (x, y, z + side(c), 1 - c))
    )
    masses = [
        receive(mass, lambda x, y, z, c, step=step: (x + step, y, z, c)) if step else mass for step in STEPS
    ]
    return finish(pos, masses)


def solution(mesh):
    devices = Mesh(np.asarray(mesh.devices).reshape(SIZES), AXES)
    return jax.shard_map(
        shards, mesh=devices, in_specs=(P(AXES, None), P(AXES)), out_specs=P(AXES), check_vma=False
    )
```

```python
import functools

import jax
import jax.numpy as jnp
import numpy as np
from jax import lax
from jax.experimental import pallas as pl
from jax.experimental.pallas import tpu as pltpu
from jax.sharding import Mesh
from jax.sharding import PartitionSpec as P

CL_GRP = 64
GROUPS = 4
TEMP = 0.05
RATE = 1.4426950408889634 / TEMP
STEPS = (0, 1, 3, 2)
AXES = ("x", "y", "z", "c")
SIZES = (4, 4, 4, 2)
TAIL = 8
VMEM_LIMIT = 32 * 1024 * 1024


def iotas(rows, cols):
    return (
        lax.broadcasted_iota(jnp.int32, (rows, cols), 0),
        lax.broadcasted_iota(jnp.int32, (rows, cols), 1),
    )


def as_column(row):
    n = row.shape[1]
    down, across = iotas(n, n)
    return jnp.sum(jnp.where(down == across, row, 0.0), axis=1, keepdims=True)


def prepare_kernel(x_ref, emb_hbm, ids_hbm, c0_ref, c1_ref, c3_ref, c2_ref, pos_ref, emb_ref, ids_ref, sems):
    emb_copy = pltpu.make_async_copy(emb_hbm, emb_ref, sems.at[0])
    ids_copy = pltpu.make_async_copy(ids_hbm, ids_ref, sems.at[1])
    emb_copy.start()
    ids_copy.start()
    rows = emb_ref.shape[0]
    share = rows // GROUPS
    down, across = iotas(rows, rows)
    ids_copy.wait()
    ids = ids_ref[...].reshape(1, rows)
    steps = (lax.shift_right_logical(ids, 6) - x_ref[0]) & (GROUPS - 1)
    slot = steps ^ lax.shift_right_logical(steps, 1)
    key = (slot * rows + across[:1]).astype(jnp.float32)
    pos = jnp.sum(jnp.where(as_column(key) < key, 1.0, 0.0), axis=0, keepdims=True)
    pos_ref[...] = pos
    place = jnp.where(down.astype(jnp.float32) == pos, 1.0, 0.0).astype(jnp.bfloat16)
    wide = jnp.broadcast_to(ids.astype(jnp.float32), (TAIL, rows)).astype(jnp.bfloat16)
    placed_ids = lax.dot_general(
        wide, place, (((1,), (1,)), ((), ())), preferred_element_type=jnp.float32
    )
    emb_copy.wait()
    values = emb_ref[...].astype(jnp.float32)
    scale = lax.rsqrt(jnp.sum(values * values, axis=1, keepdims=True) + 1e-06)
    units = (values * scale).astype(jnp.bfloat16)
    placed = jnp.dot(place, units, preferred_element_type=jnp.float32).astype(jnp.bfloat16)
    chunk_of = lax.broadcasted_iota(jnp.int32, (TAIL, rows), 1)
    for k, out in enumerate((c0_ref, c1_ref, c3_ref, c2_ref)):
        out[:share, :] = placed[k * share : (k + 1) * share]
        here = (chunk_of >= k * share) & (chunk_of < (k + 1) * share)
        out[share:, :rows] = jnp.where(here, placed_ids, 0.0).astype(jnp.bfloat16)
        out[share:, rows:] = jnp.zeros((TAIL, out.shape[1] - rows), jnp.bfloat16)


def prepare(x_index, embeddings, ids):
    rows, width = embeddings.shape
    share = rows // GROUPS
    chunk = jax.ShapeDtypeStruct((share + TAIL, width), jnp.bfloat16)
    return pl.pallas_call(
        prepare_kernel,
        out_shape=[chunk] * GROUPS + [jax.ShapeDtypeStruct((1, rows), jnp.float32)],
        in_specs=[
            pl.BlockSpec(memory_space=pltpu.SMEM),
            pl.BlockSpec(memory_space=pltpu.HBM),
            pl.BlockSpec(memory_space=pltpu.HBM),
        ],
        scratch_shapes=[
            pltpu.VMEM((rows, width), jnp.bfloat16),
            pltpu.VMEM((rows,), jnp.int32),
            pltpu.SemaphoreType.DMA((2,)),
        ],
        compiler_params=pltpu.CompilerParams(vmem_limit_bytes=VMEM_LIMIT),
        name="prepare",
    )(x_index, *(pltpu.with_memory_space_constraint(a, pltpu.HBM) for a in (embeddings, ids)))


def join_kernel(c0_ref, c1_ref, c2_ref, c3_ref, out_ref):
    chunks = (c0_ref, c1_ref, c2_ref, c3_ref)
    share = c0_ref.shape[0] - TAIL
    tail = 0.0
    for k, chunk in enumerate(chunks):
        out_ref[k * share : (k + 1) * share, :] = chunk[:share, :]
        tail += chunk[share:, :].astype(jnp.float32)
    out_ref[GROUPS * share :, :] = tail.astype(jnp.bfloat16)


def join(chunks):
    share = chunks[0].shape[0] - TAIL
    return pl.pallas_call(
        join_kernel,
        out_shape=jax.ShapeDtypeStruct((GROUPS * share + TAIL, chunks[0].shape[1]), jnp.bfloat16),
        compiler_params=pltpu.CompilerParams(vmem_limit_bytes=VMEM_LIMIT),
        name="join",
    )(*chunks)


def pairs_kernel(nq, nk, plan, *refs):
    queries, keys = refs[:nq], refs[nq : nq + nk]
    out_ref, down_acc, across_acc = refs[nq + nk :]
    rows = out_ref.shape[2]
    down_acc[...] = jnp.zeros_like(down_acc)
    across_acc[...] = jnp.zeros_like(across_acc)

    def id_rows(blocks):
        return [block[rows:, :rows][:1].astype(jnp.float32) for block in blocks]

    def id_column(block):
        return jnp.transpose(jnp.broadcast_to(id_rows([block])[0], (128, rows)))

    def similar(tall, wide):
        parts = [block[:rows, :] for block in wide]
        return lax.dot_general(
            tall[:rows, :],
            jnp.concatenate(parts, axis=0) if len(parts) > 1 else parts[0],
            (((1,), (1,)), ((), ())),
            preferred_element_type=jnp.float32,
        )

    def term(similarity, keep):
        return jnp.where(keep, jnp.exp2((similarity - 1.0) * RATE), 0.0)

    for qs, ks, *same in plan:
        if len(ks) == 1:
            similarity = similar(keys[ks[0]], [queries[q] for q in qs])
            key_ids = id_column(keys[ks[0]])
            for i, (q, query_ids) in enumerate(zip(qs, id_rows([queries[q] for q in qs]))):
                for lane in range(0, rows, 128):
                    tile = similarity[:, i * rows + lane : i * rows + lane + 128]
                    terms = term(tile, key_ids == query_ids[:, lane : lane + 128])
                    down_acc[:, q * rows + lane : q * rows + lane + 128] += jnp.sum(
                        terms.reshape(rows // 8, 8, 128), axis=0
                    )
        else:
            (q,) = qs
            similarity = similar(queries[q], [keys[k] for k in ks])
            query_ids = id_column(queries[q])
            total = across_acc[q]
            for i, key_ids in enumerate(id_rows([keys[k] for k in ks])):
                for lane in range(0, rows, 128):
                    tile = similarity[:, i * rows + lane : i * rows + lane + 128]
                    keep = query_ids == key_ids[:, lane : lane + 128]
                    if same and i == 0:
                        down, across = iotas(rows, 128)
                        keep = keep & (down != across + lane)
                    total += term(tile, keep)
            across_acc[q] = total
    across_used = {qs[0] for qs, ks, *_ in plan if len(ks) > 1}
    for q in range(nq):
        total = jnp.sum(down_acc[:, q * rows : (q + 1) * rows], axis=0, keepdims=True)
        if q in across_used:
            total += jnp.sum(jnp.transpose(across_acc[q]), axis=0, keepdims=True)
        out_ref[q] = total


def pair_sums(queries, keys, plan, name):
    rows, width = queries[0].shape[0] - TAIL, queries[0].shape[1]
    nq, nk = len(queries), len(keys)
    products = sum(len(qs) * len(ks) for qs, ks, *_ in plan) * rows * rows
    return pl.pallas_call(
        functools.partial(pairs_kernel, nq, nk, plan),
        out_shape=jax.ShapeDtypeStruct((nq, 1, rows), jnp.float32),
        in_specs=[pl.BlockSpec(memory_space=pltpu.VMEM)] * (nq + nk),
        out_specs=pl.BlockSpec(memory_space=pltpu.VMEM),
        scratch_shapes=[
            pltpu.VMEM((8, nq * rows), jnp.float32),
            pltpu.VMEM((nq, rows, 128), jnp.float32),
        ],
        compiler_params=pltpu.CompilerParams(vmem_limit_bytes=VMEM_LIMIT),
        cost_estimate=pl.CostEstimate(
            flops=2 * products * width,
            bytes_accessed=(nq + nk) * rows * width * 2,
            transcendentals=products,
        ),
        name=name,
    )(*queries, *keys)


def finish_kernel(pos_ref, m0_ref, m1_ref, m2_ref, m3_ref, out_ref):
    rows = pos_ref.shape[1]
    share = rows // GROUPS
    lane = lax.broadcasted_iota(jnp.int32, (1, rows), 1)
    masses = m0_ref[...]
    for k, ref in enumerate((m1_ref, m2_ref, m3_ref), 1):
        masses = jnp.where(lane >= k * share, ref[...], masses)
    down, _ = iotas(rows, rows)
    picked = jnp.where(down.astype(jnp.float32) == pos_ref[...], as_column(masses), 0.0)
    out_ref[...] = jnp.log1p(jnp.sum(picked, axis=0))


def finish(pos, masses):
    return pl.pallas_call(
        finish_kernel,
        out_shape=jax.ShapeDtypeStruct((pos.shape[1],), jnp.float32),
        compiler_params=pltpu.CompilerParams(vmem_limit_bytes=VMEM_LIMIT),
        name="finish",
    )(pos, *masses)


def pairs_of(source_of):
    moves = []
    for here in np.ndindex(*SIZES):
        there = tuple(int(v) % n for v, n in zip(source_of(*here), SIZES))
        moves.append((int(np.ravel_multi_index(there, SIZES)), int(np.ravel_multi_index(here, SIZES))))
    return moves


def receive(array, source_of):
    return lax.ppermute(array, AXES, pairs_of(source_of))


def side(c):
    return -1 if c == 0 else 1


def swap(a):
    return receive(a, lambda x, y, z, c: (x, y, z, 1 - c))


def near_y(a):
    return receive(a, lambda x, y, z, c: (x, y + side(c), z, c))


def near_z(a):
    return receive(a, lambda x, y, z, c: (x, y, z + side(c), c))


def shards(embeddings, cluster_ids):
    rows = embeddings.shape[0]
    x_index = lax.axis_index("x").astype(jnp.int32).reshape(1)
    *chunks, pos = prepare(x_index, embeddings, cluster_ids)
    for k, step in enumerate(STEPS):
        if step:
            chunks[k] = receive(chunks[k], lambda x, y, z, c, step=step: (x - step, y, z, c))
    own = join(chunks)

    az, ay = lax.optimization_barrier((near_z(own), near_y(own)))
    other = swap(own)
    fz, fy = near_z(az), near_y(ay)
    bz, by = lax.optimization_barrier((near_z(other), near_y(other)))
    ay2, by2 = swap(ay), swap(by)
    s1 = pair_sums(
        [az, bz, own],
        [own, other, ay, ay2, by],
        (
            ((0, 1), (0,)),
            ((0, 1), (1,)),
            ((0, 1), (2,)),
            ((0, 1), (3,)),
            ((0, 1), (4,)),
            ((2,), (0, 1), True),
            ((2,), (2, 3)),
        ),
        name="pairs_a",
    )
    fy, s1 = lax.optimization_barrier((fy, s1))
    fy2 = swap(fy)
    s2 = pair_sums([az, bz], [by2, fy], (((0, 1), (0,)), ((0, 1), (1,))), name="pairs_b")
    s3 = pair_sums(
        [az, bz, fz],
        [own, other, ay, ay2, by, by2, fy, fy2],
        (((2,), (0, 1)), ((2,), (2, 3)), ((2,), (4, 5)), ((2,), (6, 7)), ((0, 1), (7,))),
        name="pairs_f",
    )
    s0 = pair_sums([own], [by, by2, fy, fy2], (((0,), (0, 1)), ((0,), (2, 3))), name="pairs_own")
    mass_a = s1[0] + s2[0] + s3[0]
    mass_b = s1[1] + s2[1] + s3[1]
    mass_f = s3[2]
    mass = (
        s0[0]
        + s1[2]
        + receive(mass_f, lambda x, y, z, c: (x, y, z + 2, c))
        + receive(mass_a, lambda x, y, z, c: (x, y, z - side(c), c))
        + receive(mass_b, lambda x, y, z, c: (x, y, z + side(c), 1 - c))
    )
    masses = [
        receive(mass, lambda x, y, z, c, step=step: (x + step, y, z, c)) if step else mass for step in STEPS
    ]
    return finish(pos, masses)


def solution(mesh):
    devices = Mesh(np.asarray(mesh.devices).reshape(SIZES), AXES)
    return jax.shard_map(
        shards, mesh=devices, in_specs=(P(AXES, None), P(AXES)), out_specs=P(AXES), check_vma=False
    )
```

```python
import functools

import jax
import jax.numpy as jnp
import numpy as np
from jax import lax
from jax.experimental import pallas as pl
from jax.experimental.pallas import tpu as pltpu
from jax.sharding import Mesh
from jax.sharding import PartitionSpec as P

CL_GRP = 64
GROUPS = 4
TEMP = 0.05
RATE = 1.4426950408889634 / TEMP
STEPS = (0, 1, 3, 2)
AXES = ("x", "y", "z", "c")
SIZES = (4, 4, 4, 2)
TAIL = 8
VMEM_LIMIT = 32 * 1024 * 1024


def iotas(rows, cols):
    return (
        lax.broadcasted_iota(jnp.int32, (rows, cols), 0),
        lax.broadcasted_iota(jnp.int32, (rows, cols), 1),
    )


def as_column(row):
    n = row.shape[1]
    down, across = iotas(n, n)
    return jnp.sum(jnp.where(down == across, row, 0.0), axis=1, keepdims=True)


def prepare_kernel(x_ref, emb_hbm, ids_hbm, c0_ref, c1_ref, c3_ref, c2_ref, pos_ref, emb_ref, ids_ref, sems):
    emb_copy = pltpu.make_async_copy(emb_hbm, emb_ref, sems.at[0])
    ids_copy = pltpu.make_async_copy(ids_hbm, ids_ref, sems.at[1])
    emb_copy.start()
    ids_copy.start()
    rows = emb_ref.shape[0]
    share = rows // GROUPS
    down, across = iotas(rows, rows)
    ids_copy.wait()
    ids = ids_ref[...].reshape(1, rows)
    steps = (lax.shift_right_logical(ids, 6) - x_ref[0]) & (GROUPS - 1)
    slot = steps ^ lax.shift_right_logical(steps, 1)
    key = (slot * rows + across[:1]).astype(jnp.float32)
    pos = jnp.sum(jnp.where(as_column(key) < key, 1.0, 0.0), axis=0, keepdims=True)
    pos_ref[...] = pos
    place = jnp.where(down.astype(jnp.float32) == pos, 1.0, 0.0).astype(jnp.bfloat16)
    wide = jnp.broadcast_to(ids.astype(jnp.float32), (TAIL, rows)).astype(jnp.bfloat16)
    placed_ids = lax.dot_general(
        wide, place, (((1,), (1,)), ((), ())), preferred_element_type=jnp.float32
    )
    emb_copy.wait()
    values = emb_ref[...].astype(jnp.float32)
    scale = lax.rsqrt(jnp.sum(values * values, axis=1, keepdims=True) + 1e-06)
    units = (values * scale).astype(jnp.bfloat16)
    placed = jnp.dot(place, units, preferred_element_type=jnp.float32).astype(jnp.bfloat16)
    chunk_of = lax.broadcasted_iota(jnp.int32, (TAIL, rows), 1)
    for k, out in enumerate((c0_ref, c1_ref, c3_ref, c2_ref)):
        out[:share, :] = placed[k * share : (k + 1) * share]
        here = (chunk_of >= k * share) & (chunk_of < (k + 1) * share)
        out[share:, :rows] = jnp.where(here, placed_ids, 0.0).astype(jnp.bfloat16)
        out[share:, rows:] = jnp.zeros((TAIL, out.shape[1] - rows), jnp.bfloat16)


def prepare(x_index, embeddings, ids):
    rows, width = embeddings.shape
    share = rows // GROUPS
    chunk = jax.ShapeDtypeStruct((share + TAIL, width), jnp.bfloat16)
    return pl.pallas_call(
        prepare_kernel,
        out_shape=[chunk] * GROUPS + [jax.ShapeDtypeStruct((1, rows), jnp.float32)],
        in_specs=[
            pl.BlockSpec(memory_space=pltpu.SMEM),
            pl.BlockSpec(memory_space=pltpu.HBM),
            pl.BlockSpec(memory_space=pltpu.HBM),
        ],
        scratch_shapes=[
            pltpu.VMEM((rows, width), jnp.bfloat16),
            pltpu.VMEM((rows,), jnp.int32),
            pltpu.SemaphoreType.DMA((2,)),
        ],
        compiler_params=pltpu.CompilerParams(vmem_limit_bytes=VMEM_LIMIT),
        name="prepare",
    )(x_index, *(pltpu.with_memory_space_constraint(a, pltpu.HBM) for a in (embeddings, ids)))


def join_kernel(c0_ref, c1_ref, c2_ref, c3_ref, out_ref):
    chunks = (c0_ref, c1_ref, c2_ref, c3_ref)
    share = c0_ref.shape[0] - TAIL
    tail = 0.0
    for k, chunk in enumerate(chunks):
        out_ref[k * share : (k + 1) * share, :] = chunk[:share, :]
        tail += chunk[share:, :].astype(jnp.float32)
    out_ref[GROUPS * share :, :] = tail.astype(jnp.bfloat16)


def join(chunks):
    share = chunks[0].shape[0] - TAIL
    return pl.pallas_call(
        join_kernel,
        out_shape=jax.ShapeDtypeStruct((GROUPS * share + TAIL, chunks[0].shape[1]), jnp.bfloat16),
        compiler_params=pltpu.CompilerParams(vmem_limit_bytes=VMEM_LIMIT),
        name="join",
    )(*chunks)


def pairs_kernel(nq, nk, plan, *refs):
    queries, keys = refs[:nq], refs[nq : nq + nk]
    out_ref, down_acc, across_acc = refs[nq + nk :]
    rows = out_ref.shape[2]
    down_acc[...] = jnp.zeros_like(down_acc)
    across_acc[...] = jnp.zeros_like(across_acc)

    def id_rows(blocks):
        return [block[rows:, :rows][:1].astype(jnp.float32) for block in blocks]

    def id_column(block):
        return jnp.transpose(jnp.broadcast_to(id_rows([block])[0], (128, rows)))

    def similar(tall, wide):
        parts = [block[:rows, :] for block in wide]
        return lax.dot_general(
            tall[:rows, :],
            jnp.concatenate(parts, axis=0) if len(parts) > 1 else parts[0],
            (((1,), (1,)), ((), ())),
            preferred_element_type=jnp.float32,
        )

    def term(similarity, keep):
        return jnp.where(keep, jnp.exp2((similarity - 1.0) * RATE), 0.0)

    for qs, ks, *same in plan:
        if len(ks) == 1:
            similarity = similar(keys[ks[0]], [queries[q] for q in qs])
            key_ids = id_column(keys[ks[0]])
            for i, (q, query_ids) in enumerate(zip(qs, id_rows([queries[q] for q in qs]))):
                for lane in range(0, rows, 128):
                    tile = similarity[:, i * rows + lane : i * rows + lane + 128]
                    terms = term(tile, key_ids == query_ids[:, lane : lane + 128])
                    down_acc[:, q * rows + lane : q * rows + lane + 128] += jnp.sum(
                        terms.reshape(rows // 8, 8, 128), axis=0
                    )
        else:
            (q,) = qs
            similarity = similar(queries[q], [keys[k] for k in ks])
            query_ids = id_column(queries[q])
            total = across_acc[q]
            for i, key_ids in enumerate(id_rows([keys[k] for k in ks])):
                for lane in range(0, rows, 128):
                    tile = similarity[:, i * rows + lane : i * rows + lane + 128]
                    keep = query_ids == key_ids[:, lane : lane + 128]
                    if same and i == 0:
                        down, across = iotas(rows, 128)
                        keep = keep & (down != across + lane)
                    total += term(tile, keep)
            across_acc[q] = total
    across_used = {qs[0] for qs, ks, *_ in plan if len(ks) > 1}
    for q in range(nq):
        total = jnp.sum(down_acc[:, q * rows : (q + 1) * rows], axis=0, keepdims=True)
        if q in across_used:
            total += jnp.sum(jnp.transpose(across_acc[q]), axis=0, keepdims=True)
        out_ref[q] = total


def pair_sums(queries, keys, plan, name):
    rows, width = queries[0].shape[0] - TAIL, queries[0].shape[1]
    nq, nk = len(queries), len(keys)
    products = sum(len(qs) * len(ks) for qs, ks, *_ in plan) * rows * rows
    return pl.pallas_call(
        functools.partial(pairs_kernel, nq, nk, plan),
        out_shape=jax.ShapeDtypeStruct((nq, 1, rows), jnp.float32),
        in_specs=[pl.BlockSpec(memory_space=pltpu.VMEM)] * (nq + nk),
        out_specs=pl.BlockSpec(memory_space=pltpu.VMEM),
        scratch_shapes=[
            pltpu.VMEM((8, nq * rows), jnp.float32),
            pltpu.VMEM((nq, rows, 128), jnp.float32),
        ],
        compiler_params=pltpu.CompilerParams(vmem_limit_bytes=VMEM_LIMIT),
        cost_estimate=pl.CostEstimate(
            flops=2 * products * width,
            bytes_accessed=(nq + nk) * rows * width * 2,
            transcendentals=products,
        ),
        name=name,
    )(*queries, *keys)


def finish_kernel(pos_ref, m0_ref, m1_ref, m2_ref, m3_ref, out_ref):
    rows = pos_ref.shape[1]
    share = rows // GROUPS
    lane = lax.broadcasted_iota(jnp.int32, (1, rows), 1)
    masses = m0_ref[...]
    for k, ref in enumerate((m1_ref, m2_ref, m3_ref), 1):
        masses = jnp.where(lane >= k * share, ref[...], masses)
    down, _ = iotas(rows, rows)
    picked = jnp.where(down.astype(jnp.float32) == pos_ref[...], as_column(masses), 0.0)
    out_ref[...] = jnp.log1p(jnp.sum(picked, axis=0))


def finish(pos, masses):
    return pl.pallas_call(
        finish_kernel,
        out_shape=jax.ShapeDtypeStruct((pos.shape[1],), jnp.float32),
        compiler_params=pltpu.CompilerParams(vmem_limit_bytes=VMEM_LIMIT),
        name="finish",
    )(pos, *masses)


def pairs_of(source_of):
    moves = []
    for here in np.ndindex(*SIZES):
        there = tuple(int(v) % n for v, n in zip(source_of(*here), SIZES))
        moves.append((int(np.ravel_multi_index(there, SIZES)), int(np.ravel_multi_index(here, SIZES))))
    return moves


def receive(array, source_of):
    return lax.ppermute(array, AXES, pairs_of(source_of))


def side(c):
    return -1 if c == 0 else 1


def swap(a):
    return receive(a, lambda x, y, z, c: (x, y, z, 1 - c))


def near_y(a):
    return receive(a, lambda x, y, z, c: (x, y + side(c), z, c))


def near_z(a):
    return receive(a, lambda x, y, z, c: (x, y, z + side(c), c))


def shards(embeddings, cluster_ids):
    rows = embeddings.shape[0]
    x_index = lax.axis_index("x").astype(jnp.int32).reshape(1)
    *chunks, pos = prepare(x_index, embeddings, cluster_ids)
    for k, step in enumerate(STEPS):
        if step:
            chunks[k] = receive(chunks[k], lambda x, y, z, c, step=step: (x - step, y, z, c))
    own = join(chunks)

    az, ay = near_z(own), near_y(own)
    other = swap(own)
    fz, fy = near_z(az), near_y(ay)
    bz, by = lax.optimization_barrier((near_z(other), near_y(other)))
    ay2, by2 = swap(ay), swap(by)
    s1 = pair_sums(
        [az, bz, own],
        [own, other, ay, ay2, by],
        (
            ((0, 1), (0,)),
            ((0, 1), (1,)),
            ((0, 1), (2,)),
            ((0, 1), (3,)),
            ((0, 1), (4,)),
            ((2,), (0, 1), True),
            ((2,), (2, 3)),
        ),
        name="pairs_a",
    )
    fy, s1 = lax.optimization_barrier((fy, s1))
    fy2 = swap(fy)
    s2 = pair_sums([az, bz], [by2, fy], (((0, 1), (0,)), ((0, 1), (1,))), name="pairs_b")
    s3 = pair_sums(
        [az, bz, fz],
        [own, other, ay, ay2, by, by2, fy, fy2],
        (((2,), (0, 1)), ((2,), (2, 3)), ((2,), (4, 5)), ((2,), (6, 7)), ((0, 1), (7,))),
        name="pairs_f",
    )
    s0 = pair_sums([own], [by, by2, fy, fy2], (((0,), (0, 1)), ((0,), (2, 3))), name="pairs_own")
    mass_a = s1[0] + s2[0] + s3[0]
    mass_b = s1[1] + s2[1] + s3[1]
    mass_f = s3[2]
    mass = (
        s0[0]
        + s1[2]
        + receive(mass_f, lambda x, y, z, c: (x, y, z + 2, c))
        + receive(mass_a, lambda x, y, z, c: (x, y, z - side(c), c))
        + receive(mass_b, lambda x, y, z, c: (x, y, z + side(c), 1 - c))
    )
    masses = [
        receive(mass, lambda x, y, z, c, step=step: (x + step, y, z, c)) if step else mass for step in STEPS
    ]
    return finish(pos, masses)


def solution(mesh):
    devices = Mesh(np.asarray(mesh.devices).reshape(SIZES), AXES)
    return jax.shard_map(
        shards, mesh=devices, in_specs=(P(AXES, None), P(AXES)), out_specs=P(AXES), check_vma=False
    )
```

```python
import functools

import jax
import jax.numpy as jnp
import numpy as np
from jax import lax
from jax.experimental import pallas as pl
from jax.experimental.pallas import tpu as pltpu
from jax.sharding import Mesh
from jax.sharding import PartitionSpec as P

CL_GRP = 64
GROUPS = 4
TEMP = 0.05
RATE = 1.4426950408889634 / TEMP
STEPS = (0, 1, 3, 2)
AXES = ("x", "y", "z", "c")
SIZES = (4, 4, 4, 2)
TAIL = 8
VMEM_LIMIT = 32 * 1024 * 1024


def iotas(rows, cols):
    return (
        lax.broadcasted_iota(jnp.int32, (rows, cols), 0),
        lax.broadcasted_iota(jnp.int32, (rows, cols), 1),
    )


def as_column(row):
    n = row.shape[1]
    down, across = iotas(n, n)
    return jnp.sum(jnp.where(down == across, row, 0.0), axis=1, keepdims=True)


def prepare_kernel(x_ref, emb_hbm, ids_hbm, c0_ref, c1_ref, c3_ref, c2_ref, pos_ref, emb_ref, ids_ref, sems):
    emb_copy = pltpu.make_async_copy(emb_hbm, emb_ref, sems.at[0])
    ids_copy = pltpu.make_async_copy(ids_hbm, ids_ref, sems.at[1])
    emb_copy.start()
    ids_copy.start()
    rows = emb_ref.shape[0]
    share = rows // GROUPS
    down, across = iotas(rows, rows)
    ids_copy.wait()
    ids = ids_ref[...].reshape(1, rows)
    steps = (lax.shift_right_logical(ids, 6) - x_ref[0]) & (GROUPS - 1)
    slot = steps ^ lax.shift_right_logical(steps, 1)
    key = (slot * rows + across[:1]).astype(jnp.float32)
    pos = jnp.sum(jnp.where(as_column(key) < key, 1.0, 0.0), axis=0, keepdims=True)
    pos_ref[...] = pos
    place = jnp.where(down.astype(jnp.float32) == pos, 1.0, 0.0).astype(jnp.bfloat16)
    wide = jnp.broadcast_to(ids.astype(jnp.float32), (TAIL, rows)).astype(jnp.bfloat16)
    placed_ids = lax.dot_general(
        wide, place, (((1,), (1,)), ((), ())), preferred_element_type=jnp.float32
    )
    emb_copy.wait()
    values = emb_ref[...].astype(jnp.float32)
    scale = lax.rsqrt(jnp.sum(values * values, axis=1, keepdims=True) + 1e-06)
    units = (values * scale).astype(jnp.bfloat16)
    placed = jnp.dot(place, units, preferred_element_type=jnp.float32).astype(jnp.bfloat16)
    chunk_of = lax.broadcasted_iota(jnp.int32, (TAIL, rows), 1)
    for k, out in enumerate((c0_ref, c1_ref, c3_ref, c2_ref)):
        out[:share, :] = placed[k * share : (k + 1) * share]
        here = (chunk_of >= k * share) & (chunk_of < (k + 1) * share)
        out[share:, :rows] = jnp.where(here, placed_ids, 0.0).astype(jnp.bfloat16)
        out[share:, rows:] = jnp.zeros((TAIL, out.shape[1] - rows), jnp.bfloat16)


def prepare(x_index, embeddings, ids):
    rows, width = embeddings.shape
    share = rows // GROUPS
    chunk = jax.ShapeDtypeStruct((share + TAIL, width), jnp.bfloat16)
    return pl.pallas_call(
        prepare_kernel,
        out_shape=[chunk] * GROUPS + [jax.ShapeDtypeStruct((1, rows), jnp.float32)],
        in_specs=[
            pl.BlockSpec(memory_space=pltpu.SMEM),
            pl.BlockSpec(memory_space=pltpu.HBM),
            pl.BlockSpec(memory_space=pltpu.HBM),
        ],
        scratch_shapes=[
            pltpu.VMEM((rows, width), jnp.bfloat16),
            pltpu.VMEM((rows,), jnp.int32),
            pltpu.SemaphoreType.DMA((2,)),
        ],
        compiler_params=pltpu.CompilerParams(vmem_limit_bytes=VMEM_LIMIT),
        name="prepare",
    )(x_index, *(pltpu.with_memory_space_constraint(a, pltpu.HBM) for a in (embeddings, ids)))


def join_kernel(c0_ref, c1_ref, c2_ref, c3_ref, out_ref):
    chunks = (c0_ref, c1_ref, c2_ref, c3_ref)
    share = c0_ref.shape[0] - TAIL
    tail = 0.0
    for k, chunk in enumerate(chunks):
        out_ref[k * share : (k + 1) * share, :] = chunk[:share, :]
        tail += chunk[share:, :].astype(jnp.float32)
    out_ref[GROUPS * share :, :] = tail.astype(jnp.bfloat16)


def join(chunks):
    share = chunks[0].shape[0] - TAIL
    return pl.pallas_call(
        join_kernel,
        out_shape=jax.ShapeDtypeStruct((GROUPS * share + TAIL, chunks[0].shape[1]), jnp.bfloat16),
        compiler_params=pltpu.CompilerParams(vmem_limit_bytes=VMEM_LIMIT),
        name="join",
    )(*chunks)


def pairs_kernel(nq, nk, plan, *refs):
    queries, keys = refs[:nq], refs[nq : nq + nk]
    out_ref, down_acc, across_acc = refs[nq + nk :]
    rows = out_ref.shape[2]
    down_acc[...] = jnp.zeros_like(down_acc)
    across_acc[...] = jnp.zeros_like(across_acc)

    def id_rows(blocks):
        return [block[rows:, :rows][:1].astype(jnp.float32) for block in blocks]

    def id_column(block):
        return jnp.transpose(jnp.broadcast_to(id_rows([block])[0], (128, rows)))

    def similar(tall, wide):
        parts = [block[:rows, :] for block in wide]
        return lax.dot_general(
            tall[:rows, :],
            jnp.concatenate(parts, axis=0) if len(parts) > 1 else parts[0],
            (((1,), (1,)), ((), ())),
            preferred_element_type=jnp.float32,
        )

    def term(similarity, keep):
        return jnp.where(keep, jnp.exp2((similarity - 1.0) * RATE), 0.0)

    for qs, ks, *same in plan:
        if len(ks) == 1:
            similarity = similar(keys[ks[0]], [queries[q] for q in qs])
            key_ids = id_column(keys[ks[0]])
            for i, (q, query_ids) in enumerate(zip(qs, id_rows([queries[q] for q in qs]))):
                for lane in range(0, rows, 128):
                    tile = similarity[:, i * rows + lane : i * rows + lane + 128]
                    terms = term(tile, key_ids == query_ids[:, lane : lane + 128])
                    down_acc[:, q * rows + lane : q * rows + lane + 128] += jnp.sum(
                        terms.reshape(rows // 8, 8, 128), axis=0
                    )
        else:
            (q,) = qs
            similarity = similar(queries[q], [keys[k] for k in ks])
            query_ids = id_column(queries[q])
            total = across_acc[q]
            for i, key_ids in enumerate(id_rows([keys[k] for k in ks])):
                for lane in range(0, rows, 128):
                    tile = similarity[:, i * rows + lane : i * rows + lane + 128]
                    keep = query_ids == key_ids[:, lane : lane + 128]
                    if same and i == 0:
                        down, across = iotas(rows, 128)
                        keep = keep & (down != across + lane)
                    total += term(tile, keep)
            across_acc[q] = total
    across_used = {qs[0] for qs, ks, *_ in plan if len(ks) > 1}
    for q in range(nq):
        total = jnp.sum(down_acc[:, q * rows : (q + 1) * rows], axis=0, keepdims=True)
        if q in across_used:
            total += jnp.sum(jnp.transpose(across_acc[q]), axis=0, keepdims=True)
        out_ref[q] = total


def pair_sums(queries, keys, plan, name):
    rows, width = queries[0].shape[0] - TAIL, queries[0].shape[1]
    nq, nk = len(queries), len(keys)
    products = sum(len(qs) * len(ks) for qs, ks, *_ in plan) * rows * rows
    return pl.pallas_call(
        functools.partial(pairs_kernel, nq, nk, plan),
        out_shape=jax.ShapeDtypeStruct((nq, 1, rows), jnp.float32),
        in_specs=[pl.BlockSpec(memory_space=pltpu.VMEM)] * (nq + nk),
        out_specs=pl.BlockSpec(memory_space=pltpu.VMEM),
        scratch_shapes=[
            pltpu.VMEM((8, nq * rows), jnp.float32),
            pltpu.VMEM((nq, rows, 128), jnp.float32),
        ],
        compiler_params=pltpu.CompilerParams(vmem_limit_bytes=VMEM_LIMIT),
        cost_estimate=pl.CostEstimate(
            flops=2 * products * width,
            bytes_accessed=(nq + nk) * rows * width * 2,
            transcendentals=products,
        ),
        name=name,
    )(*queries, *keys)


def finish_kernel(pos_ref, m0_ref, m1_ref, m2_ref, m3_ref, out_ref):
    rows = pos_ref.shape[1]
    share = rows // GROUPS
    lane = lax.broadcasted_iota(jnp.int32, (1, rows), 1)
    masses = m0_ref[...]
    for k, ref in enumerate((m1_ref, m2_ref, m3_ref), 1):
        masses = jnp.where(lane >= k * share, ref[...], masses)
    down, _ = iotas(rows, rows)
    picked = jnp.where(down.astype(jnp.float32) == pos_ref[...], as_column(masses), 0.0)
    out_ref[...] = jnp.log1p(jnp.sum(picked, axis=0))


def finish(pos, masses):
    return pl.pallas_call(
        finish_kernel,
        out_shape=jax.ShapeDtypeStruct((pos.shape[1],), jnp.float32),
        compiler_params=pltpu.CompilerParams(vmem_limit_bytes=VMEM_LIMIT),
        name="finish",
    )(pos, *masses)


def pairs_of(source_of):
    moves = []
    for here in np.ndindex(*SIZES):
        there = tuple(int(v) % n for v, n in zip(source_of(*here), SIZES))
        moves.append((int(np.ravel_multi_index(there, SIZES)), int(np.ravel_multi_index(here, SIZES))))
    return moves


def receive(array, source_of):
    return lax.ppermute(array, AXES, pairs_of(source_of))


def side(c):
    return -1 if c == 0 else 1


def swap(a):
    return receive(a, lambda x, y, z, c: (x, y, z, 1 - c))


def near_y(a):
    return receive(a, lambda x, y, z, c: (x, y + side(c), z, c))


def near_z(a):
    return receive(a, lambda x, y, z, c: (x, y, z + side(c), c))


def shards(embeddings, cluster_ids):
    rows = embeddings.shape[0]
    x_index = lax.axis_index("x").astype(jnp.int32).reshape(1)
    *chunks, pos = prepare(x_index, embeddings, cluster_ids)
    for k, step in enumerate(STEPS):
        if step:
            chunks[k] = receive(chunks[k], lambda x, y, z, c, step=step: (x - step, y, z, c))
    own = join(chunks)

    az, ay = near_z(own), near_y(own)
    other = swap(own)
    fz, fy = near_z(az), near_y(ay)
    bz, by = lax.optimization_barrier((near_z(other), near_y(other)))
    ay2, by2 = swap(ay), swap(by)
    s1 = pair_sums(
        [az, bz],
        [own, other, ay, ay2, by],
        (((0, 1), (0,)), ((0, 1), (1,)), ((0, 1), (2,)), ((0, 1), (3,)), ((0, 1), (4,))),
        name="pairs_a",
    )
    fy, s1 = lax.optimization_barrier((fy, s1))
    fy2 = swap(fy)
    s2 = pair_sums([az, bz], [by2, fy], (((0, 1), (0,)), ((0, 1), (1,))), name="pairs_b")
    s3 = pair_sums(
        [az, bz, fz],
        [own, other, ay, ay2, by, by2, fy, fy2],
        (((2,), (0, 1)), ((2,), (2, 3)), ((2,), (4, 5)), ((2,), (6, 7)), ((0, 1), (7,))),
        name="pairs_f",
    )
    s0 = pair_sums(
        [own],
        [own, other, ay, ay2, by, by2, fy, fy2],
        (((0,), (0, 1), True), ((0,), (2, 3)), ((0,), (4, 5)), ((0,), (6, 7))),
        name="pairs_own",
    )
    mass_a = s1[0] + s2[0] + s3[0]
    mass_b = s1[1] + s2[1] + s3[1]
    mass_f = s3[2]
    mass = (
        s0[0]
        + receive(mass_f, lambda x, y, z, c: (x, y, z + 2, c))
        + receive(mass_a, lambda x, y, z, c: (x, y, z - side(c), c))
        + receive(mass_b, lambda x, y, z, c: (x, y, z + side(c), 1 - c))
    )
    masses = [
        receive(mass, lambda x, y, z, c, step=step: (x + step, y, z, c)) if step else mass for step in STEPS
    ]
    return finish(pos, masses)


def solution(mesh):
    devices = Mesh(np.asarray(mesh.devices).reshape(SIZES), AXES)
    return jax.shard_map(
        shards, mesh=devices, in_specs=(P(AXES, None), P(AXES)), out_specs=P(AXES), check_vma=False
    )
```

```python
import functools

import jax
import jax.numpy as jnp
import numpy as np
from jax import lax
from jax.experimental import pallas as pl
from jax.experimental.pallas import tpu as pltpu
from jax.sharding import Mesh
from jax.sharding import PartitionSpec as P

CL_GRP = 64
GROUPS = 4
TEMP = 0.05
RATE = 1.4426950408889634 / TEMP
STEPS = (0, 1, 3, 2)
AXES = ("x", "y", "z", "c")
SIZES = (4, 4, 4, 2)
TAIL = 8
VMEM_LIMIT = 32 * 1024 * 1024


def iotas(rows, cols):
    return (
        lax.broadcasted_iota(jnp.int32, (rows, cols), 0),
        lax.broadcasted_iota(jnp.int32, (rows, cols), 1),
    )


def as_column(row):
    n = row.shape[1]
    down, across = iotas(n, n)
    return jnp.sum(jnp.where(down == across, row, 0.0), axis=1, keepdims=True)


def prepare_kernel(x_ref, emb_hbm, ids_hbm, c0_ref, c1_ref, c3_ref, c2_ref, pos_ref, emb_ref, ids_ref, sems):
    emb_copy = pltpu.make_async_copy(emb_hbm, emb_ref, sems.at[0])
    ids_copy = pltpu.make_async_copy(ids_hbm, ids_ref, sems.at[1])
    emb_copy.start()
    ids_copy.start()
    rows = emb_ref.shape[0]
    share = rows // GROUPS
    down, across = iotas(rows, rows)
    ids_copy.wait()
    ids = ids_ref[...].reshape(1, rows)
    steps = (lax.shift_right_logical(ids, 6) - x_ref[0]) & (GROUPS - 1)
    slot = steps ^ lax.shift_right_logical(steps, 1)
    key = (slot * rows + across[:1]).astype(jnp.float32)
    pos = jnp.sum(jnp.where(as_column(key) < key, 1.0, 0.0), axis=0, keepdims=True)
    pos_ref[...] = pos
    place = jnp.where(down.astype(jnp.float32) == pos, 1.0, 0.0).astype(jnp.bfloat16)
    wide = jnp.broadcast_to(ids.astype(jnp.float32), (TAIL, rows)).astype(jnp.bfloat16)
    placed_ids = lax.dot_general(
        wide, place, (((1,), (1,)), ((), ())), preferred_element_type=jnp.float32
    )
    emb_copy.wait()
    values = emb_ref[...].astype(jnp.float32)
    scale = lax.rsqrt(jnp.sum(values * values, axis=1, keepdims=True) + 1e-06)
    units = (values * scale).astype(jnp.bfloat16)
    placed = jnp.dot(place, units, preferred_element_type=jnp.float32).astype(jnp.bfloat16)
    chunk_of = lax.broadcasted_iota(jnp.int32, (TAIL, rows), 1)
    for k, out in enumerate((c0_ref, c1_ref, c3_ref, c2_ref)):
        out[:share, :] = placed[k * share : (k + 1) * share]
        here = (chunk_of >= k * share) & (chunk_of < (k + 1) * share)
        out[share:, :rows] = jnp.where(here, placed_ids, 0.0).astype(jnp.bfloat16)
        out[share:, rows:] = jnp.zeros((TAIL, out.shape[1] - rows), jnp.bfloat16)


def prepare(x_index, embeddings, ids):
    rows, width = embeddings.shape
    share = rows // GROUPS
    chunk = jax.ShapeDtypeStruct((share + TAIL, width), jnp.bfloat16)
    return pl.pallas_call(
        prepare_kernel,
        out_shape=[chunk] * GROUPS + [jax.ShapeDtypeStruct((1, rows), jnp.float32)],
        in_specs=[
            pl.BlockSpec(memory_space=pltpu.SMEM),
            pl.BlockSpec(memory_space=pltpu.HBM),
            pl.BlockSpec(memory_space=pltpu.HBM),
        ],
        scratch_shapes=[
            pltpu.VMEM((rows, width), jnp.bfloat16),
            pltpu.VMEM((rows,), jnp.int32),
            pltpu.SemaphoreType.DMA((2,)),
        ],
        compiler_params=pltpu.CompilerParams(vmem_limit_bytes=VMEM_LIMIT),
        name="prepare",
    )(x_index, *(pltpu.with_memory_space_constraint(a, pltpu.HBM) for a in (embeddings, ids)))


def join_kernel(c0_ref, c1_ref, c2_ref, c3_ref, out_ref):
    chunks = (c0_ref, c1_ref, c2_ref, c3_ref)
    share = c0_ref.shape[0] - TAIL
    tail = 0.0
    for k, chunk in enumerate(chunks):
        out_ref[k * share : (k + 1) * share, :] = chunk[:share, :]
        tail += chunk[share:, :].astype(jnp.float32)
    out_ref[GROUPS * share :, :] = tail.astype(jnp.bfloat16)


def join(chunks):
    share = chunks[0].shape[0] - TAIL
    return pl.pallas_call(
        join_kernel,
        out_shape=jax.ShapeDtypeStruct((GROUPS * share + TAIL, chunks[0].shape[1]), jnp.bfloat16),
        compiler_params=pltpu.CompilerParams(vmem_limit_bytes=VMEM_LIMIT),
        name="join",
    )(*chunks)


def pairs_kernel(nq, nk, plan, *refs):
    queries, keys = refs[:nq], refs[nq : nq + nk]
    out_ref, down_acc, across_acc = refs[nq + nk :]
    rows = out_ref.shape[2]
    down_acc[...] = jnp.zeros_like(down_acc)
    across_acc[...] = jnp.zeros_like(across_acc)

    def id_rows(blocks):
        return [block[rows:, :rows][:1].astype(jnp.float32) for block in blocks]

    def id_column(block):
        return jnp.transpose(jnp.broadcast_to(id_rows([block])[0], (128, rows)))

    def similar(tall, wide):
        parts = [block[:rows, :] for block in wide]
        return lax.dot_general(
            tall[:rows, :],
            jnp.concatenate(parts, axis=0) if len(parts) > 1 else parts[0],
            (((1,), (1,)), ((), ())),
            preferred_element_type=jnp.float32,
        )

    def term(similarity, keep):
        return jnp.where(keep, jnp.exp2((similarity - 1.0) * RATE), 0.0)

    for qs, ks, *same in plan:
        if len(ks) == 1:
            similarity = similar(keys[ks[0]], [queries[q] for q in qs])
            key_ids = id_column(keys[ks[0]])
            for i, (q, query_ids) in enumerate(zip(qs, id_rows([queries[q] for q in qs]))):
                for lane in range(0, rows, 128):
                    tile = similarity[:, i * rows + lane : i * rows + lane + 128]
                    terms = term(tile, key_ids == query_ids[:, lane : lane + 128])
                    down_acc[:, q * rows + lane : q * rows + lane + 128] += jnp.sum(
                        terms.reshape(rows // 8, 8, 128), axis=0
                    )
        else:
            (q,) = qs
            similarity = similar(queries[q], [keys[k] for k in ks])
            query_ids = id_column(queries[q])
            total = across_acc[q]
            for i, key_ids in enumerate(id_rows([keys[k] for k in ks])):
                for lane in range(0, rows, 128):
                    tile = similarity[:, i * rows + lane : i * rows + lane + 128]
                    keep = query_ids == key_ids[:, lane : lane + 128]
                    if same and i == 0:
                        down, across = iotas(rows, 128)
                        keep = keep & (down != across + lane)
                    total += term(tile, keep)
            across_acc[q] = total
    across_used = {qs[0] for qs, ks, *_ in plan if len(ks) > 1}
    for q in range(nq):
        total = jnp.sum(down_acc[:, q * rows : (q + 1) * rows], axis=0, keepdims=True)
        if q in across_used:
            total += jnp.sum(jnp.transpose(across_acc[q]), axis=0, keepdims=True)
        out_ref[q] = total


def pair_sums(queries, keys, plan, name):
    rows, width = queries[0].shape[0] - TAIL, queries[0].shape[1]
    nq, nk = len(queries), len(keys)
    products = sum(len(qs) * len(ks) for qs, ks, *_ in plan) * rows * rows
    return pl.pallas_call(
        functools.partial(pairs_kernel, nq, nk, plan),
        out_shape=jax.ShapeDtypeStruct((nq, 1, rows), jnp.float32),
        in_specs=[pl.BlockSpec(memory_space=pltpu.VMEM)] * (nq + nk),
        out_specs=pl.BlockSpec(memory_space=pltpu.VMEM),
        scratch_shapes=[
            pltpu.VMEM((8, nq * rows), jnp.float32),
            pltpu.VMEM((nq, rows, 128), jnp.float32),
        ],
        compiler_params=pltpu.CompilerParams(vmem_limit_bytes=VMEM_LIMIT),
        cost_estimate=pl.CostEstimate(
            flops=2 * products * width,
            bytes_accessed=(nq + nk) * rows * width * 2,
            transcendentals=products,
        ),
        name=name,
    )(*queries, *keys)


def finish_kernel(pos_ref, m0_ref, m1_ref, m2_ref, m3_ref, out_ref):
    rows = pos_ref.shape[1]
    share = rows // GROUPS
    lane = lax.broadcasted_iota(jnp.int32, (1, rows), 1)
    masses = m0_ref[...]
    for k, ref in enumerate((m1_ref, m2_ref, m3_ref), 1):
        masses = jnp.where(lane >= k * share, ref[...], masses)
    down, _ = iotas(rows, rows)
    picked = jnp.where(down.astype(jnp.float32) == pos_ref[...], as_column(masses), 0.0)
    out_ref[...] = jnp.log1p(jnp.sum(picked, axis=0))


def finish(pos, masses):
    return pl.pallas_call(
        finish_kernel,
        out_shape=jax.ShapeDtypeStruct((pos.shape[1],), jnp.float32),
        compiler_params=pltpu.CompilerParams(vmem_limit_bytes=VMEM_LIMIT),
        name="finish",
    )(pos, *masses)


def pairs_of(source_of):
    moves = []
    for here in np.ndindex(*SIZES):
        there = tuple(int(v) % n for v, n in zip(source_of(*here), SIZES))
        moves.append((int(np.ravel_multi_index(there, SIZES)), int(np.ravel_multi_index(here, SIZES))))
    return moves


def receive(array, source_of):
    return lax.ppermute(array, AXES, pairs_of(source_of))


def side(c):
    return -1 if c == 0 else 1


def swap(a):
    return receive(a, lambda x, y, z, c: (x, y, z, 1 - c))


def near_y(a):
    return receive(a, lambda x, y, z, c: (x, y + side(c), z, c))


def near_z(a):
    return receive(a, lambda x, y, z, c: (x, y, z + side(c), c))


def shards(embeddings, cluster_ids):
    rows = embeddings.shape[0]
    x_index = lax.axis_index("x").astype(jnp.int32).reshape(1)
    *chunks, pos = prepare(x_index, embeddings, cluster_ids)
    for k, step in enumerate(STEPS):
        if step:
            chunks[k] = receive(chunks[k], lambda x, y, z, c, step=step: (x - step, y, z, c))
    own = join(chunks)

    az, ay = near_z(own), near_y(own)
    other = swap(own)
    fz, fy = near_z(az), near_y(ay)
    bz, by = lax.optimization_barrier((near_z(other), near_y(other)))
    ay2, by2 = swap(ay), swap(by)
    s1 = pair_sums(
        [az, bz],
        [own, other, ay, ay2, by],
        (((0, 1), (0,)), ((0, 1), (1,)), ((0, 1), (2,)), ((0, 1), (3,)), ((0, 1), (4,))),
        name="pairs_a",
    )
    fy, s1 = lax.optimization_barrier((fy, s1))
    fy2 = swap(fy)
    s2 = pair_sums([az, bz], [by2, fy], (((0, 1), (0,)), ((0, 1), (1,))), name="pairs_b")
    s3 = pair_sums(
        [az, bz, fz],
        [own, other, ay, ay2, by, by2, fy, fy2],
        (((2,), (0, 1)), ((2,), (2, 3)), ((2,), (4, 5)), ((2,), (6, 7)), ((0, 1), (7,))),
        name="pairs_f",
    )
    s0 = pair_sums(
        [own],
        [own, other, ay, ay2, by, by2, fy, fy2],
        (((0,), (0, 1), True), ((0,), (2, 3)), ((0,), (4, 5)), ((0,), (6, 7))),
        name="pairs_own",
    )
    near = receive(s1 + s2 + s3[:2], lambda x, y, z, c: (x, y, z - side(c), c))
    far = receive(s3[2], lambda x, y, z, c: (x, y, z + 2, c))
    mass = s0[0] + near[0] + swap(near[1]) + far
    masses = [
        receive(mass, lambda x, y, z, c, step=step: (x + step, y, z, c)) if step else mass for step in STEPS
    ]
    return finish(pos, masses)


def solution(mesh):
    devices = Mesh(np.asarray(mesh.devices).reshape(SIZES), AXES)
    return jax.shard_map(
        shards, mesh=devices, in_specs=(P(AXES, None), P(AXES)), out_specs=P(AXES), check_vma=False
    )
```

```python
import functools

import jax
import jax.numpy as jnp
import numpy as np
from jax import lax
from jax.experimental import pallas as pl
from jax.experimental.pallas import tpu as pltpu
from jax.sharding import Mesh
from jax.sharding import PartitionSpec as P

CL_GRP = 64
GROUPS = 4
TEMP = 0.05
RATE = 1.4426950408889634 / TEMP
STEPS = (0, 1, 3, 2)
AXES = ("x", "y", "z", "c")
SIZES = (4, 4, 4, 2)
TAIL = 8
VMEM_LIMIT = 32 * 1024 * 1024


def iotas(rows, cols):
    return (
        lax.broadcasted_iota(jnp.int32, (rows, cols), 0),
        lax.broadcasted_iota(jnp.int32, (rows, cols), 1),
    )


def as_column(row):
    n = row.shape[1]
    down, across = iotas(n, n)
    return jnp.sum(jnp.where(down == across, row, 0.0), axis=1, keepdims=True)


def prepare_kernel(x_ref, emb_hbm, ids_hbm, c0_ref, c1_ref, c3_ref, c2_ref, pos_ref, emb_ref, ids_ref, sems):
    emb_copy = pltpu.make_async_copy(emb_hbm, emb_ref, sems.at[0])
    ids_copy = pltpu.make_async_copy(ids_hbm, ids_ref, sems.at[1])
    emb_copy.start()
    ids_copy.start()
    rows = emb_ref.shape[0]
    share = rows // GROUPS
    down, across = iotas(rows, rows)
    ids_copy.wait()
    ids = ids_ref[...].reshape(1, rows)
    steps = (lax.shift_right_logical(ids, 6) - x_ref[0]) & (GROUPS - 1)
    slot = steps ^ lax.shift_right_logical(steps, 1)
    key = (slot * rows + across[:1]).astype(jnp.float32)
    pos = jnp.sum(jnp.where(as_column(key) < key, 1.0, 0.0), axis=0, keepdims=True)
    pos_ref[...] = pos
    place = jnp.where(down.astype(jnp.float32) == pos, 1.0, 0.0).astype(jnp.bfloat16)
    wide = jnp.broadcast_to(ids.astype(jnp.float32), (TAIL, rows)).astype(jnp.bfloat16)
    placed_ids = lax.dot_general(
        wide, place, (((1,), (1,)), ((), ())), preferred_element_type=jnp.float32
    )
    emb_copy.wait()
    values = emb_ref[...].astype(jnp.float32)
    scale = lax.rsqrt(jnp.sum(values * values, axis=1, keepdims=True) + 1e-06)
    units = (values * scale).astype(jnp.bfloat16)
    placed = jnp.dot(place, units, preferred_element_type=jnp.float32).astype(jnp.bfloat16)
    chunk_of = lax.broadcasted_iota(jnp.int32, (TAIL, rows), 1)
    for k, out in enumerate((c0_ref, c1_ref, c3_ref, c2_ref)):
        out[:share, :] = placed[k * share : (k + 1) * share]
        here = (chunk_of >= k * share) & (chunk_of < (k + 1) * share)
        out[share:, :rows] = jnp.where(here, placed_ids, 0.0).astype(jnp.bfloat16)
        out[share:, rows:] = jnp.zeros((TAIL, out.shape[1] - rows), jnp.bfloat16)


def prepare(x_index, embeddings, ids):
    rows, width = embeddings.shape
    share = rows // GROUPS
    chunk = jax.ShapeDtypeStruct((share + TAIL, width), jnp.bfloat16)
    return pl.pallas_call(
        prepare_kernel,
        out_shape=[chunk] * GROUPS + [jax.ShapeDtypeStruct((1, rows), jnp.float32)],
        in_specs=[
            pl.BlockSpec(memory_space=pltpu.SMEM),
            pl.BlockSpec(memory_space=pltpu.HBM),
            pl.BlockSpec(memory_space=pltpu.HBM),
        ],
        scratch_shapes=[
            pltpu.VMEM((rows, width), jnp.bfloat16),
            pltpu.VMEM((rows,), jnp.int32),
            pltpu.SemaphoreType.DMA((2,)),
        ],
        compiler_params=pltpu.CompilerParams(vmem_limit_bytes=VMEM_LIMIT),
        name="prepare",
    )(x_index, *(pltpu.with_memory_space_constraint(a, pltpu.HBM) for a in (embeddings, ids)))


def join_kernel(c0_ref, c1_ref, c2_ref, c3_ref, out_ref):
    chunks = (c0_ref, c1_ref, c2_ref, c3_ref)
    share = c0_ref.shape[0] - TAIL
    tail = 0.0
    for k, chunk in enumerate(chunks):
        out_ref[k * share : (k + 1) * share, :] = chunk[:share, :]
        tail += chunk[share:, :].astype(jnp.float32)
    out_ref[GROUPS * share :, :] = tail.astype(jnp.bfloat16)


def join(chunks):
    share = chunks[0].shape[0] - TAIL
    return pl.pallas_call(
        join_kernel,
        out_shape=jax.ShapeDtypeStruct((GROUPS * share + TAIL, chunks[0].shape[1]), jnp.bfloat16),
        compiler_params=pltpu.CompilerParams(vmem_limit_bytes=VMEM_LIMIT),
        name="join",
    )(*chunks)


def pairs_kernel(nq, nk, plan, *refs):
    queries, keys = refs[:nq], refs[nq : nq + nk]
    out_ref, down_acc, across_acc = refs[nq + nk :]
    rows = out_ref.shape[2]
    down_acc[...] = jnp.zeros_like(down_acc)
    across_acc[...] = jnp.zeros_like(across_acc)

    def id_rows(blocks):
        return [block[rows:, :rows][:1].astype(jnp.float32) for block in blocks]

    def id_column(block):
        return jnp.transpose(jnp.broadcast_to(id_rows([block])[0], (128, rows)))

    def similar(tall, wide):
        parts = [block[:rows, :] for block in wide]
        return lax.dot_general(
            tall[:rows, :],
            jnp.concatenate(parts, axis=0) if len(parts) > 1 else parts[0],
            (((1,), (1,)), ((), ())),
            preferred_element_type=jnp.float32,
        )

    def term(similarity, keep):
        return jnp.where(keep, jnp.exp2((similarity - 1.0) * RATE), 0.0)

    for qs, ks, *same in plan:
        if len(ks) == 1:
            similarity = similar(keys[ks[0]], [queries[q] for q in qs])
            key_ids = id_column(keys[ks[0]])
            for i, (q, query_ids) in enumerate(zip(qs, id_rows([queries[q] for q in qs]))):
                for lane in range(0, rows, 128):
                    tile = similarity[:, i * rows + lane : i * rows + lane + 128]
                    terms = term(tile, key_ids == query_ids[:, lane : lane + 128])
                    down_acc[:, q * rows + lane : q * rows + lane + 128] += jnp.sum(
                        terms.reshape(rows // 8, 8, 128), axis=0
                    )
        else:
            (q,) = qs
            similarity = similar(queries[q], [keys[k] for k in ks])
            query_ids = id_column(queries[q])
            total = across_acc[q]
            for i, key_ids in enumerate(id_rows([keys[k] for k in ks])):
                for lane in range(0, rows, 128):
                    tile = similarity[:, i * rows + lane : i * rows + lane + 128]
                    keep = query_ids == key_ids[:, lane : lane + 128]
                    if same and i == 0:
                        down, across = iotas(rows, 128)
                        keep = keep & (down != across + lane)
                    total += term(tile, keep)
            across_acc[q] = total
    across_used = {qs[0] for qs, ks, *_ in plan if len(ks) > 1}
    for q in range(nq):
        total = jnp.sum(down_acc[:, q * rows : (q + 1) * rows], axis=0, keepdims=True)
        if q in across_used:
            total += jnp.sum(jnp.transpose(across_acc[q]), axis=0, keepdims=True)
        out_ref[q] = total


def pair_sums(queries, keys, plan, name):
    rows, width = queries[0].shape[0] - TAIL, queries[0].shape[1]
    nq, nk = len(queries), len(keys)
    products = sum(len(qs) * len(ks) for qs, ks, *_ in plan) * rows * rows
    return pl.pallas_call(
        functools.partial(pairs_kernel, nq, nk, plan),
        out_shape=jax.ShapeDtypeStruct((nq, 1, rows), jnp.float32),
        in_specs=[pl.BlockSpec(memory_space=pltpu.VMEM)] * (nq + nk),
        out_specs=pl.BlockSpec(memory_space=pltpu.VMEM),
        scratch_shapes=[
            pltpu.VMEM((8, nq * rows), jnp.float32),
            pltpu.VMEM((nq, rows, 128), jnp.float32),
        ],
        compiler_params=pltpu.CompilerParams(vmem_limit_bytes=VMEM_LIMIT),
        cost_estimate=pl.CostEstimate(
            flops=2 * products * width,
            bytes_accessed=(nq + nk) * rows * width * 2,
            transcendentals=products,
        ),
        name=name,
    )(*queries, *keys)


def finish_kernel(pos_ref, m0_ref, m1_ref, m2_ref, m3_ref, out_ref):
    rows = pos_ref.shape[1]
    share = rows // GROUPS
    lane = lax.broadcasted_iota(jnp.int32, (1, rows), 1)
    masses = m0_ref[...]
    for k, ref in enumerate((m1_ref, m2_ref, m3_ref), 1):
        masses = jnp.where(lane >= k * share, ref[...], masses)
    down, _ = iotas(rows, rows)
    picked = jnp.where(down.astype(jnp.float32) == pos_ref[...], as_column(masses), 0.0)
    out_ref[...] = jnp.log1p(jnp.sum(picked, axis=0))


def finish(pos, masses):
    return pl.pallas_call(
        finish_kernel,
        out_shape=jax.ShapeDtypeStruct((pos.shape[1],), jnp.float32),
        compiler_params=pltpu.CompilerParams(vmem_limit_bytes=VMEM_LIMIT),
        name="finish",
    )(pos, *masses)


def pairs_of(source_of):
    moves = []
    for here in np.ndindex(*SIZES):
        there = tuple(int(v) % n for v, n in zip(source_of(*here), SIZES))
        moves.append((int(np.ravel_multi_index(there, SIZES)), int(np.ravel_multi_index(here, SIZES))))
    return moves


def receive(array, source_of):
    return lax.ppermute(array, AXES, pairs_of(source_of))


def side(c):
    return -1 if c == 0 else 1


def swap(a):
    return receive(a, lambda x, y, z, c: (x, y, z, 1 - c))


def near_y(a):
    return receive(a, lambda x, y, z, c: (x, y + side(c), z, c))


def near_z(a):
    return receive(a, lambda x, y, z, c: (x, y, z + side(c), c))


def shards(embeddings, cluster_ids):
    rows = embeddings.shape[0]
    x_index = lax.axis_index("x").astype(jnp.int32).reshape(1)
    *chunks, pos = prepare(x_index, embeddings, cluster_ids)
    for k, step in enumerate(STEPS):
        if step:
            chunks[k] = receive(chunks[k], lambda x, y, z, c, step=step: (x - step, y, z, c))
    own = join(chunks)

    ay, az = near_y(own), near_z(own)
    other = swap(own)
    fy, fz = near_y(ay), near_z(az)
    bz, by = lax.optimization_barrier((near_z(other), near_y(other)))
    ay2, by2 = swap(ay), swap(by)
    s1 = pair_sums(
        [az, bz],
        [own, other, ay, ay2, by],
        (((0, 1), (0,)), ((0, 1), (1,)), ((0, 1), (2,)), ((0, 1), (3,)), ((0, 1), (4,))),
        name="pairs_a",
    )
    fy, s1 = lax.optimization_barrier((fy, s1))
    fy2 = swap(fy)
    s2 = pair_sums([az, bz], [by2, fy], (((0, 1), (0,)), ((0, 1), (1,))), name="pairs_b")
    s3 = pair_sums(
        [az, bz, fz],
        [own, other, ay, ay2, by, by2, fy, fy2],
        (((2,), (0, 1)), ((2,), (2, 3)), ((2,), (4, 5)), ((2,), (6, 7)), ((0, 1), (7,))),
        name="pairs_f",
    )
    s0 = pair_sums(
        [own],
        [own, other, ay, ay2, by, by2, fy, fy2],
        (((0,), (0, 1), True), ((0,), (2, 3)), ((0,), (4, 5)), ((0,), (6, 7))),
        name="pairs_own",
    )
    mass_a = s1[0] + s2[0] + s3[0]
    mass_b = s1[1] + s2[1] + s3[1]
    mass_f = s3[2]
    mass = (
        s0[0]
        + receive(mass_f, lambda x, y, z, c: (x, y, z + 2, c))
        + receive(mass_a, lambda x, y, z, c: (x, y, z - side(c), c))
        + receive(mass_b, lambda x, y, z, c: (x, y, z + side(c), 1 - c))
    )
    masses = [
        receive(mass, lambda x, y, z, c, step=step: (x + step, y, z, c)) if step else mass for step in STEPS
    ]
    return finish(pos, masses)


def solution(mesh):
    devices = Mesh(np.asarray(mesh.devices).reshape(SIZES), AXES)
    return jax.shard_map(
        shards, mesh=devices, in_specs=(P(AXES, None), P(AXES)), out_specs=P(AXES), check_vma=False
    )
```
